32 devices in a mesh: rep: 8 (over z, core), fsdp: 4 (over y, x).
Axes of the slice: x: 2, y: 2, z: 4, core: 2. Of those that a mesh axis runs over, the one named last changes fastest.
Arguments:
- tokens: bfloat16 [16384, 2048], P(('rep', 'fsdp')), may hold values from -6 to 6
- out_grad: bfloat16 [16384, 256], P(('rep', 'fsdp')), may hold values from -6 to 6
- gain: float32 [8, 128], P('rep'), may hold values from 0.3 to 3
- inner_weight: float32 [8, 2048, 256], P('rep', 'fsdp'), may hold values from -6 to 6
- outer_weight: float32 [8, 2048, 256], P('rep', 'fsdp'), may hold values from -6.3 to 6.3
- momentum: float32 [8, 2048, 256], P('rep', 'fsdp'), may hold values from -1.2 to 1.2
- adam_m: float32 [8, 2048, 256], P('rep', 'fsdp'), may hold values from -2 to 2
- adam_v: float32 [8, 2048, 256], P('rep', 'fsdp'), may hold values from 0.5 to 8
- gossip_offset: int32 [1], replicated, may hold values from 0 to 65535
Outputs:
- outer_new: float32 [8, 2048, 256], P('rep', 'fsdp')
- momentum_new: float32 [8, 2048, 256], P('rep', 'fsdp')
- adam_m_new: float32 [8, 2048, 256], P('rep', 'fsdp')
- adam_v_new: float32 [8, 2048, 256], P('rep', 'fsdp')
The draws below stay inside these ranges and needn't reach their ends.
All inputs are finite; a program needn't handle non-finite values.
Results may differ from the reference program's by a relative error of at most 0.0038.
Values may be sent and summed in bfloat16 or wider, within the bound.
A program may use at most 64 MiB of HBM per device.

```python
import math
import jax
import jax.numpy as jnp
from jax import lax

D = 2048
HEAD = 128
ADAM_STEP = 100
KV = 256
TOKENS = 16384
N_REP = 8


def paired_weights(key):
    folded = jax.random.fold_in(key, 4242)
    key_base, key_drift = jax.random.split(folded)
    full_shape = (N_REP, D, KV)
    base_weight = jnp.clip(jax.random.normal(key_base, full_shape, jnp.float32), -6.0, 6.0)
    drift = 0.05 * jnp.clip(jax.random.normal(key_drift, full_shape, jnp.float32), -4.0, 4.0)
    return (base_weight, base_weight + drift)


def draw_inner_weight(key, part):
    return paired_weights(key)[0]


def draw_outer_weight(key, part):
    return paired_weights(key)[1]


def shard_levels(own_key, extent, pieces, smallest, top_value):
    def one(axis_at, parts):
        draws = jax.random.uniform(jax.random.fold_in(jax.random.fold_in(own_key, 6), axis_at), (parts,), jnp.float32, smallest / len(pieces), top_value / len(pieces))
        return jnp.repeat(jnp.exp(draws), extent[axis_at] // parts).reshape((-1,) + (1,) * (len(extent) - axis_at - 1))

    level = one(*pieces[0])
    for cut in pieces[1:]:
        level = level * one(*cut)
    return level


def scatter_about(own_key, shape, spread, bound, pieces=(), kind=jnp.bfloat16):
    drawn = spread * jax.random.normal(own_key, shape, jnp.float32)
    if pieces:
        drawn = drawn * shard_levels(own_key, shape, pieces, -0.22, 0.18)
    return jnp.clip(drawn, -bound, bound).astype(kind)


def setup_inputs(seed: int = 0) -> dict:
    splits = jax.random.split(jax.random.key(seed), 10)
    return {
        "tokens": scatter_about(splits[0], (TOKENS, D), 1.0, 6.0, ((0, 32),)),
        "out_grad": scatter_about(splits[1], (TOKENS, KV), 1.0, 6.0, ((0, 32),)),
        "gain": jnp.clip(jnp.exp(math.log(3.0) - 2.3025851 * jax.random.uniform(splits[2], (N_REP, HEAD), jnp.float32) ** shard_levels(splits[2], (N_REP, HEAD), ((0, 8),), -0.2, 0.2)), 0.3, 3.0),
        "inner_weight": draw_inner_weight(jax.random.fold_in(splits[9], 71), 0),
        "outer_weight": draw_outer_weight(jax.random.fold_in(splits[9], 71), 0),
        "momentum": scatter_about(splits[5], (N_REP, D, KV), 0.2, 1.2, ((0, 8), (1, 4)), jnp.float32),
        "adam_m": scatter_about(splits[6], (N_REP, D, KV), 0.3, 2.0, ((0, 8), (1, 4)), jnp.float32),
        "adam_v": jnp.clip(jnp.exp(math.log(8.0) - 2.7725887 * jax.random.uniform(splits[7], (N_REP, D, KV), jnp.float32) ** shard_levels(splits[7], (N_REP, D, KV), ((0, 8), (1, 4)), -0.2, 0.2)), 0.5, 8.0),
        "gossip_offset": jax.random.randint(splits[8], (1,), 0, 65536).astype(jnp.int32),
    }


def replica_step(items):
    rows_x, rows_g, gain_row, inner, outer, first, second = items
    w_bf = inner.astype(jnp.bfloat16)
    keys = jnp.dot(rows_x, w_bf, preferred_element_type=jnp.float32)
    heads = keys.reshape(keys.shape[0], -1, HEAD)
    scale = lax.rsqrt(lax.optimization_barrier(jnp.mean(heads * heads, axis=-1, keepdims=True)) + 1e-06)
    unit = heads * scale
    g_out = rows_g.astype(jnp.float32).reshape(heads.shape) * gain_row
    inner_prod = lax.optimization_barrier(jnp.mean(unit * g_out, axis=-1, keepdims=True))
    key_grad = (scale * (g_out - unit * inner_prod)).reshape(keys.shape).astype(jnp.bfloat16)
    grad = jnp.dot(rows_x.T, key_grad, preferred_element_type=jnp.float32)
    first_new = 0.9 * first + 0.1 * grad
    second_new = 0.95 * second + 0.05 * grad * grad
    fix_one = 1.0 - 0.9 ** ADAM_STEP
    fix_two = 1.0 - 0.95 ** ADAM_STEP
    update = first_new / fix_one / (jnp.sqrt(second_new / fix_two) + 1e-08) + 0.1 * inner
    inner_next = inner - 0.05 * update
    delta = outer - inner_next
    return (first_new, second_new, delta)

def reference(tokens, out_grad, gain, inner_weight, outer_weight, momentum, adam_m, adam_v, gossip_offset):
    per_rep = tokens.shape[0] // N_REP
    rows_x = tokens.reshape(N_REP, per_rep, tokens.shape[1])
    rows_g = out_grad.reshape(N_REP, per_rep, out_grad.shape[1])
    first_new, second_new, delta = lax.map(replica_step, (rows_x, rows_g, gain, inner_weight, outer_weight, adam_m, adam_v))
    index = jnp.arange(N_REP, dtype=jnp.int32)
    offset = (1 + gossip_offset[0].astype(jnp.int32) % (N_REP - 1)).astype(jnp.int32)
    partner = ((index - offset) % N_REP).astype(jnp.int32)
    mean_delta = (delta + delta[partner]) / 2.0
    momentum_new = 0.9 * momentum + mean_delta
    outer_new = (outer_weight + outer_weight[partner]) / 2.0 - 0.7 * (0.9 * momentum_new + mean_delta)
    return (outer_new, momentum_new, first_new, second_new)
```

```python
import functools

import jax
import jax.numpy as jnp
from jax import lax
from jax.experimental import pallas as pl
from jax.experimental.pallas import tpu as pltpu
from jax.sharding import PartitionSpec as P

HEAD = 128
ADAM_STEP = 100
FIX_ONE = 1.0 - 0.9**ADAM_STEP
FIX_TWO = 1.0 - 0.95**ADAM_STEP
CHUNKS = 4
DIRECT_REPS = 8
MESH = pl.DeviceIdType.MESH
F32 = jnp.float32
BF16 = jnp.bfloat16


def from_behind(block, axis, distance):
    devices = range(lax.axis_size(axis))
    route = [((i - distance) % len(devices), i) for i in devices]
    return lax.ppermute(block, axis, route)


def gossip(values, offset, count_rep, wire):
    current = values
    for bit in range((count_rep - 1).bit_length()):
        span = (1 << bit) % count_rep
        digit = jnp.bitwise_and(jnp.right_shift(offset, bit), 1)
        moved = from_behind(current.astype(wire), "rep", span).astype(values.dtype)
        current = jnp.where(digit != 0, moved, current)
    return current


def partners(me, k, count):
    if count & (count - 1) == 0:
        other = me
        bit = 1
        while bit < count:
            if k & bit:
                other = other + bit * (1 - 2 * lax.rem(lax.div(me, bit), 2))
            bit *= 2
        return other, other
    return lax.rem(me + k, count), lax.rem(me + count - k, count)


def kernel(
    hop, count_rep, count, *refs
):
    (tok_hbm, og_hbm, gain_ref, inner_hbm, outer_hbm, mom_hbm, first_hbm, second_hbm), refs = refs[:8], refs[8:]
    outs, refs = refs[:4] if hop else refs[:3], refs[4:] if hop else refs[3:]
    (tok, tok_t, og, inner, outer, mom, first, second, w_all, out_buf, g_send, g_recv, g_own) = refs[:13]
    (load_sem, tok_sem, ag_send, ag_recv, rs_send, rs_recv, put_sem) = refs[13:20]
    if hop:
        outer_far, outer_out, delta_far, delta_out, far_send, far_recv, d_send, d_recv = refs[20:]

    me = lax.axis_index("fsdp")
    rows = inner.shape[0]
    part = rows // CHUNKS
    order = [k for k in range(1, count)]
    send_to = {k: partners(me, k, count)[0] for k in order}
    owner = {k: partners(me, k, count)[1] for k in order}
    owner[0] = me

    barrier = pltpu.get_barrier_semaphore()
    for k in order:
        pl.semaphore_signal(barrier, inc=1, device_id={"fsdp": owner[k]}, device_id_type=MESH)
    if hop:
        rep = lax.axis_index("rep")
        ahead = lax.rem(rep + hop, count_rep)
        behind = lax.rem(rep + count_rep - hop, count_rep)
        pl.semaphore_signal(barrier, inc=1, device_id={"rep": behind}, device_id_type=MESH)

    loads = [
        pltpu.make_async_copy(src, dst, load_sem.at[i])
        for i, (src, dst) in enumerate(
            [(inner_hbm, inner), (outer_hbm, outer), (og_hbm, og), (first_hbm, first), (second_hbm, second), (mom_hbm, mom)]
        )
    ]
    tok_loads = []
    for k in range(count):
        cols = pl.ds(pl.multiple_of(owner[k] * rows, rows), rows)
        tok_loads.append(pltpu.make_async_copy(tok_hbm.at[:, cols], tok.at[k], tok_sem.at[k]))
    loads[0].start()
    loads[1].start()
    for copy in tok_loads:
        copy.start()
    for copy in loads[2:]:
        copy.start()

    loads[0].wait()
    w_all[0] = inner[...].astype(BF16)
    pl.semaphore_wait(barrier, count if hop else count - 1)
    gathers = {}
    for k in reversed(order):
        gathers[k] = pltpu.make_async_remote_copy(
            src_ref=w_all.at[0],
            dst_ref=w_all.at[k],
            send_sem=ag_send.at[k],
            recv_sem=ag_recv.at[k],
            device_id={"fsdp": send_to[k]},
            device_id_type=MESH,
        )
        gathers[k].start()
    loads[1].wait()
    if hop:
        outer_out[...] = outer[...].astype(BF16)
        far = pltpu.make_async_remote_copy(
            src_ref=outer_out,
            dst_ref=outer_far,
            send_sem=far_send.at[0],
            recv_sem=far_recv.at[0],
            device_id={"rep": ahead},
            device_id_type=MESH,
        )
        far.start()

    for k in range(count):
        tok_loads[k].wait()
        tok_t[k] = tok[k].T
    for copy in loads[2:]:
        copy.wait()
    keys = jnp.dot(tok[0], w_all[0], preferred_element_type=F32)
    for k in order:
        gathers[k].wait_recv()
        keys = keys + jnp.dot(tok[k], w_all[k], preferred_element_type=F32)

    gain = gain_ref[...]
    pieces = []
    for h in range(keys.shape[1] // HEAD):
        head = keys[:, h * HEAD : (h + 1) * HEAD]
        scale = lax.rsqrt(jnp.mean(head * head, axis=-1, keepdims=True) + 1e-06)
        unit = head * scale
        g_out = og[:, h * HEAD : (h + 1) * HEAD].astype(F32) * gain
        inner_prod = jnp.mean(unit * g_out, axis=-1, keepdims=True)
        pieces.append((scale * (g_out - unit * inner_prod)).astype(BF16))
    key_grad = jnp.concatenate(pieces, axis=1)

    sums = {}
    for c in range(CHUNKS):
        span = pl.ds(c * part, part)
        for k in list(reversed(order)) + [0]:
            term = jnp.dot(tok_t[k, span, :], key_grad, preferred_element_type=F32)
            if k == 0:
                g_own[span, :] = term
                continue
            g_send[k - 1, span, :] = term.astype(BF16)
            copy = pltpu.make_async_remote_copy(
                src_ref=g_send.at[k - 1, span, :],
                dst_ref=g_recv.at[k - 1, span, :],
                send_sem=rs_send.at[k - 1, c],
                recv_sem=rs_recv.at[k - 1, c],
                device_id={"fsdp": send_to[k]},
                device_id_type=MESH,
            )
            copy.start()
            sums[k, c] = copy

    puts = []

    def put(slot, c, values):
        span = pl.ds(c * part, part)
        out_buf[slot, span, :] = values
        copy = pltpu.make_async_copy(out_buf.at[slot, span, :], outs[slot].at[span, :], put_sem.at[slot, c])
        copy.start()
        puts.append(copy)

    hops = []
    for c in range(CHUNKS):
        span = pl.ds(c * part, part)
        grad = g_own[span, :]
        for k in order:
            sums[k, c].wait_recv()
            grad = grad + g_recv[k - 1, span, :].astype(F32)
        first_new = 0.9 * first[span, :] + 0.1 * grad
        second_new = 0.95 * second[span, :] + 0.05 * grad * grad
        held = inner[span, :]
        update = first_new / FIX_ONE / (jnp.sqrt(second_new / FIX_TWO) + 1e-08) + 0.1 * held
        delta = outer[span, :] - (held - 0.05 * update)
        if hop:
            delta_out[span, :] = delta.astype(BF16)
            copy = pltpu.make_async_remote_copy(
                src_ref=delta_out.at[span, :],
                dst_ref=delta_far.at[span, :],
                send_sem=d_send.at[c],
                recv_sem=d_recv.at[c],
                device_id={"rep": ahead},
                device_id_type=MESH,
            )
            copy.start()
            hops.append(copy)
            g_own[span, :] = delta
        else:
            put(0, c, delta)
        put(len(outs) - 2, c, first_new)
        put(len(outs) - 1, c, second_new)

    if hop:
        far.wait_recv()
        for c in range(CHUNKS):
            span = pl.ds(c * part, part)
            hops[c].wait_recv()
            mean_delta = (g_own[span, :] + delta_far[span, :].astype(F32)) / 2.0
            momentum_new = 0.9 * mom[span, :] + mean_delta
            mid = (outer[span, :] + outer_far[span, :].astype(F32)) / 2.0
            put(1, c, momentum_new)
            put(0, c, mid - 0.7 * (0.9 * momentum_new + mean_delta))

    for k in order:
        gathers[k].wait_send()
        for c in range(CHUNKS):
            sums[k, c].wait_send()
    if hop:
        far.wait_send()
        for copy in hops:
            copy.wait_send()
    for copy in puts:
        copy.wait()


def fused(hop, tokens, out_grad, gain, inner, outer, mom, first, second):
    count = lax.axis_size("fsdp")
    count_rep = lax.axis_size("rep")
    rows, width = inner.shape
    n_tok = tokens.shape[0]
    n_out = 4 if hop else 3
    full = lambda kind, *lead: pltpu.VMEM((*lead, rows, width), kind)
    dma = pltpu.SemaphoreType.DMA
    scratch = [
        pltpu.VMEM((count, n_tok, rows), BF16),
        pltpu.VMEM((count, rows, n_tok), BF16),
        pltpu.VMEM((n_tok, width), BF16),
        full(F32),
        full(F32),
        full(F32),
        full(F32),
        full(F32),
        full(BF16, count),
        full(F32, n_out),
        full(BF16, count - 1),
        full(BF16, count - 1),
        full(F32),
        dma((6,)),
        dma((count,)),
        dma((count,)),
        dma((count,)),
        dma((count - 1, CHUNKS)),
        dma((count - 1, CHUNKS)),
        dma((n_out, CHUNKS)),
    ]
    if hop:
        scratch += [full(BF16), full(BF16), full(BF16), full(BF16), dma((1,)), dma((1,)), dma((CHUNKS,)), dma((CHUNKS,))]
    hbm = pl.BlockSpec(memory_space=pl.ANY)
    return pl.pallas_call(
        functools.partial(kernel, hop, count_rep, count),
        out_shape=[jax.ShapeDtypeStruct((rows, width), F32)] * n_out,
        in_specs=[hbm, hbm, pl.BlockSpec(memory_space=pltpu.VMEM)] + [hbm] * 5,
        out_specs=[hbm] * n_out,
        scratch_shapes=scratch,
        cost_estimate=pl.CostEstimate(
            flops=4 * n_tok * rows * count * width, bytes_accessed=8 << 20, transcendentals=2 * rows * width
        ),
        compiler_params=pltpu.CompilerParams(
            collective_id=hop, has_side_effects=True, vmem_limit_bytes=48 << 20
        ),
        name=f"fused_hop{hop}",
    )(tokens, out_grad, gain, inner, outer, mom, first, second)


def local(
    tokens, out_grad, gain, inner_weight, outer_weight, momentum, adam_m, adam_v, gossip_offset
):
    count_rep = lax.axis_size("rep")
    code = gossip_offset[0] % (count_rep - 1)
    args = (tokens, out_grad, gain, inner_weight[0], outer_weight[0], momentum[0], adam_m[0], adam_v[0])
    if count_rep <= DIRECT_REPS:
        branches = [functools.partial(fused, hop) for hop in range(1, count_rep)]
        outs = lax.switch(code, branches, *args)
    else:
        offset = 1 + code
        outer = outer_weight[0]
        outer_far = gossip(outer, offset, count_rep, F32)
        delta, first_new, second_new = fused(0, *args)
        delta_far = gossip(delta, offset, count_rep, BF16)
        mean_delta = (delta + delta_far) / 2.0
        momentum_new = 0.9 * momentum[0] + mean_delta
        outer_new = (outer + outer_far) / 2.0 - 0.7 * (0.9 * momentum_new + mean_delta)
        outs = (outer_new, momentum_new, first_new, second_new)
    return tuple(out[None] for out in outs)


def solution(mesh):
    row = P("rep", "fsdp", None)
    both = P(("rep", "fsdp"), None)
    return jax.shard_map(
        local,
        mesh=mesh,
        in_specs=(both, both, P("rep", None), row, row, row, row, row, P()),
        out_specs=(row, row, row, row),
        check_vma=False,
    )
```

```python
import functools

import jax
import jax.numpy as jnp
from jax import lax
from jax.experimental import pallas as pl
from jax.experimental.pallas import tpu as pltpu
from jax.sharding import PartitionSpec as P

HEAD = 128
ADAM_STEP = 100
FIX_ONE = 1.0 - 0.9**ADAM_STEP
FIX_TWO = 1.0 - 0.95**ADAM_STEP
CHUNKS = 4
DIRECT_REPS = 8
MESH = pl.DeviceIdType.MESH
F32 = jnp.float32
BF16 = jnp.bfloat16


def from_behind(block, axis, distance):
    devices = range(lax.axis_size(axis))
    route = [((i - distance) % len(devices), i) for i in devices]
    return lax.ppermute(block, axis, route)


def gossip(values, offset, count_rep, wire):
    current = values
    for bit in range((count_rep - 1).bit_length()):
        span = (1 << bit) % count_rep
        digit = jnp.bitwise_and(jnp.right_shift(offset, bit), 1)
        moved = from_behind(current.astype(wire), "rep", span).astype(values.dtype)
        current = jnp.where(digit != 0, moved, current)
    return current


def partners(me, k, count):
    if count & (count - 1) == 0:
        other = me
        bit = 1
        while bit < count:
            if k & bit:
                other = other + bit * (1 - 2 * lax.rem(lax.div(me, bit), 2))
            bit *= 2
        return other, other
    return lax.rem(me + k, count), lax.rem(me + count - k, count)


def kernel(
    hop, count_rep, count, *refs
):
    (tok_hbm, og_hbm, gain_ref, inner_hbm, outer_hbm, mom_hbm, first_hbm, second_hbm), refs = refs[:8], refs[8:]
    outs, refs = refs[:4] if hop else refs[:3], refs[4:] if hop else refs[3:]
    (tok, tok_t, og, inner, outer, mom, first, second, w_all, out_buf, g_send, g_recv, g_own) = refs[:13]
    (load_sem, tok_sem, ag_send, ag_recv, rs_send, rs_recv, put_sem) = refs[13:20]
    if hop:
        outer_far, outer_out, delta_far, delta_out, far_send, far_recv, d_send, d_recv = refs[20:]

    me = lax.axis_index("fsdp")
    rows = inner.shape[0]
    part = rows // CHUNKS
    order = [k for k in range(1, count)]
    send_to = {k: partners(me, k, count)[0] for k in order}
    owner = {k: partners(me, k, count)[1] for k in order}
    owner[0] = me

    barrier = pltpu.get_barrier_semaphore()
    for k in order:
        pl.semaphore_signal(barrier, inc=1, device_id={"fsdp": owner[k]}, device_id_type=MESH)
    if hop:
        rep = lax.axis_index("rep")
        ahead = lax.rem(rep + hop, count_rep)
        behind = lax.rem(rep + count_rep - hop, count_rep)
        pl.semaphore_signal(barrier, inc=1, device_id={"rep": behind}, device_id_type=MESH)

    loads = [
        pltpu.make_async_copy(src, dst, load_sem.at[i])
        for i, (src, dst) in enumerate(
            [(inner_hbm, inner), (outer_hbm, outer), (og_hbm, og), (first_hbm, first), (second_hbm, second), (mom_hbm, mom)]
        )
    ]
    tok_loads = []
    for k in range(count):
        cols = pl.ds(pl.multiple_of(owner[k] * rows, rows), rows)
        tok_loads.append(pltpu.make_async_copy(tok_hbm.at[:, cols], tok.at[k], tok_sem.at[k]))
    loads[0].start()
    loads[1].start()
    for copy in tok_loads:
        copy.start()
    for copy in loads[2:]:
        copy.start()

    loads[0].wait()
    w_all[0] = inner[...].astype(BF16)
    pl.semaphore_wait(barrier, count if hop else count - 1)
    gathers = {}

    def gather(k, half, src, to):
        span = pl.ds(half * (rows // 2), rows // 2)
        gathers[k, half] = pltpu.make_async_remote_copy(
            src_ref=w_all.at[src, span, :],
            dst_ref=w_all.at[k, span, :],
            send_sem=ag_send.at[k, half],
            recv_sem=ag_recv.at[k, half],
            device_id={"fsdp": send_to[to]},
            device_id_type=MESH,
        )
        gathers[k, half].start()

    relayed = count == 4
    for half in range(2):
        for k in [1, 2] if relayed else reversed(order):
            gather(k, 1 - half if k == 1 else half, 0, k)
    loads[1].wait()
    if hop:
        outer_out[...] = outer[...].astype(BF16)
        far = pltpu.make_async_remote_copy(
            src_ref=outer_out,
            dst_ref=outer_far,
            send_sem=far_send.at[0],
            recv_sem=far_recv.at[0],
            device_id={"rep": ahead},
            device_id_type=MESH,
        )
        far.start()

    for k in range(count):
        tok_loads[k].wait()
        tok_t[k] = tok[k].T
    if relayed:
        gathers[2, 0].wait_recv()
        gather(3, 0, 2, 1)
        gathers[1, 1].wait_recv()
        gather(3, 1, 1, 2)
    for copy in loads[2:]:
        copy.wait()
    keys = jnp.dot(tok[0], w_all[0], preferred_element_type=F32)
    for k in order:
        for half in range(2):
            if not relayed or (k, half) not in ((2, 0), (1, 1)):
                gathers[k, half].wait_recv()
        keys = keys + jnp.dot(tok[k], w_all[k], preferred_element_type=F32)

    gain = gain_ref[...]
    pieces = []
    for h in range(keys.shape[1] // HEAD):
        head = keys[:, h * HEAD : (h + 1) * HEAD]
        scale = lax.rsqrt(jnp.mean(head * head, axis=-1, keepdims=True) + 1e-06)
        unit = head * scale
        g_out = og[:, h * HEAD : (h + 1) * HEAD].astype(F32) * gain
        inner_prod = jnp.mean(unit * g_out, axis=-1, keepdims=True)
        pieces.append((scale * (g_out - unit * inner_prod)).astype(BF16))
    key_grad = jnp.concatenate(pieces, axis=1)

    sums = {}
    for c in range(CHUNKS):
        span = pl.ds(c * part, part)
        for k in list(reversed(order)) + [0]:
            term = jnp.dot(tok_t[k, span, :], key_grad, preferred_element_type=F32)
            if k == 0:
                g_own[span, :] = term
                continue
            g_send[k - 1, span, :] = term.astype(BF16)
            copy = pltpu.make_async_remote_copy(
                src_ref=g_send.at[k - 1, span, :],
                dst_ref=g_recv.at[k - 1, span, :],
                send_sem=rs_send.at[k - 1, c],
                recv_sem=rs_recv.at[k - 1, c],
                device_id={"fsdp": send_to[k]},
                device_id_type=MESH,
            )
            copy.start()
            sums[k, c] = copy

    puts = []

    def put(slot, c, values):
        span = pl.ds(c * part, part)
        out_buf[slot, span, :] = values
        copy = pltpu.make_async_copy(out_buf.at[slot, span, :], outs[slot].at[span, :], put_sem.at[slot, c])
        copy.start()
        puts.append(copy)

    hops = []
    for c in range(CHUNKS):
        span = pl.ds(c * part, part)
        grad = g_own[span, :]
        for k in order:
            sums[k, c].wait_recv()
            grad = grad + g_recv[k - 1, span, :].astype(F32)
        first_new = 0.9 * first[span, :] + 0.1 * grad
        second_new = 0.95 * second[span, :] + 0.05 * grad * grad
        held = inner[span, :]
        update = first_new / FIX_ONE / (jnp.sqrt(second_new / FIX_TWO) + 1e-08) + 0.1 * held
        delta = outer[span, :] - (held - 0.05 * update)
        if hop:
            delta_out[span, :] = delta.astype(BF16)
            copy = pltpu.make_async_remote_copy(
                src_ref=delta_out.at[span, :],
                dst_ref=delta_far.at[span, :],
                send_sem=d_send.at[c],
                recv_sem=d_recv.at[c],
                device_id={"rep": ahead},
                device_id_type=MESH,
            )
            copy.start()
            hops.append(copy)
            g_own[span, :] = delta
        else:
            put(0, c, delta)
        put(len(outs) - 2, c, first_new)
        put(len(outs) - 1, c, second_new)

    if hop:
        far.wait_recv()
        for c in range(CHUNKS):
            span = pl.ds(c * part, part)
            hops[c].wait_recv()
            mean_delta = (g_own[span, :] + delta_far[span, :].astype(F32)) / 2.0
            momentum_new = 0.9 * mom[span, :] + mean_delta
            mid = (outer[span, :] + outer_far[span, :].astype(F32)) / 2.0
            put(1, c, momentum_new)
            put(0, c, mid - 0.7 * (0.9 * momentum_new + mean_delta))

    for k in order:
        for half in range(2):
            gathers[k, half].wait_send()
        for c in range(CHUNKS):
            sums[k, c].wait_send()
    if hop:
        far.wait_send()
        for copy in hops:
            copy.wait_send()
    for copy in puts:
        copy.wait()


def fused(hop, tokens, out_grad, gain, inner, outer, mom, first, second):
    count = lax.axis_size("fsdp")
    count_rep = lax.axis_size("rep")
    rows, width = inner.shape
    n_tok = tokens.shape[0]
    n_out = 4 if hop else 3
    full = lambda kind, *lead: pltpu.VMEM((*lead, rows, width), kind)
    dma = pltpu.SemaphoreType.DMA
    scratch = [
        pltpu.VMEM((count, n_tok, rows), BF16),
        pltpu.VMEM((count, rows, n_tok), BF16),
        pltpu.VMEM((n_tok, width), BF16),
        full(F32),
        full(F32),
        full(F32),
        full(F32),
        full(F32),
        full(BF16, count),
        full(F32, n_out),
        full(BF16, count - 1),
        full(BF16, count - 1),
        full(F32),
        dma((6,)),
        dma((count,)),
        dma((count, 2)),
        dma((count, 2)),
        dma((count - 1, CHUNKS)),
        dma((count - 1, CHUNKS)),
        dma((n_out, CHUNKS)),
    ]
    if hop:
        scratch += [full(BF16), full(BF16), full(BF16), full(BF16), dma((1,)), dma((1,)), dma((CHUNKS,)), dma((CHUNKS,))]
    hbm = pl.BlockSpec(memory_space=pl.ANY)
    return pl.pallas_call(
        functools.partial(kernel, hop, count_rep, count),
        out_shape=[jax.ShapeDtypeStruct((rows, width), F32)] * n_out,
        in_specs=[hbm, hbm, pl.BlockSpec(memory_space=pltpu.VMEM)] + [hbm] * 5,
        out_specs=[hbm] * n_out,
        scratch_shapes=scratch,
        cost_estimate=pl.CostEstimate(
            flops=4 * n_tok * rows * count * width, bytes_accessed=8 << 20, transcendentals=2 * rows * width
        ),
        compiler_params=pltpu.CompilerParams(
            collective_id=hop, has_side_effects=True, vmem_limit_bytes=48 << 20
        ),
        name=f"fused_hop{hop}",
    )(tokens, out_grad, gain, inner, outer, mom, first, second)


def drain(*refs):
    n = len(refs) // 2
    copies = [pltpu.make_async_copy(refs[i], refs[n + i], refs[-1].at[i]) for i in range(n)]
    for copy in copies:
        copy.start()
    for copy in copies:
        copy.wait()


def store(outs):
    hbm = pl.BlockSpec(memory_space=pl.ANY)
    return pl.pallas_call(
        drain,
        out_shape=[jax.ShapeDtypeStruct(out.shape, out.dtype) for out in outs],
        in_specs=[hbm] * len(outs),
        out_specs=[hbm] * len(outs),
        scratch_shapes=[pltpu.SemaphoreType.DMA((len(outs),))],
        name="store",
    )(*outs)


def local(
    tokens, out_grad, gain, inner_weight, outer_weight, momentum, adam_m, adam_v, gossip_offset
):
    count_rep = lax.axis_size("rep")
    code = gossip_offset[0] % (count_rep - 1)
    args = (tokens, out_grad, gain, inner_weight[0], outer_weight[0], momentum[0], adam_m[0], adam_v[0])
    if count_rep <= DIRECT_REPS:
        branches = [functools.partial(fused, hop) for hop in range(1, count_rep)]
        outs = store(lax.switch(code, branches, *args))
    else:
        offset = 1 + code
        outer = outer_weight[0]
        outer_far = gossip(outer, offset, count_rep, F32)
        delta, first_new, second_new = fused(0, *args)
        delta_far = gossip(delta, offset, count_rep, BF16)
        mean_delta = (delta + delta_far) / 2.0
        momentum_new = 0.9 * momentum[0] + mean_delta
        outer_new = (outer + outer_far) / 2.0 - 0.7 * (0.9 * momentum_new + mean_delta)
        outs = (outer_new, momentum_new, first_new, second_new)
    return tuple(out[None] for out in outs)


def solution(mesh):
    row = P("rep", "fsdp", None)
    both = P(("rep", "fsdp"), None)
    return jax.shard_map(
        local,
        mesh=mesh,
        in_specs=(both, both, P("rep", None), row, row, row, row, row, P()),
        out_specs=(row, row, row, row),
        check_vma=False,
    )
```

```python
import functools

import jax
import jax.numpy as jnp
from jax import lax
from jax.experimental import pallas as pl
from jax.experimental.pallas import tpu as pltpu
from jax.sharding import PartitionSpec as P

HEAD = 128
ADAM_STEP = 100
FIX_ONE = 1.0 - 0.9**ADAM_STEP
FIX_TWO = 1.0 - 0.95**ADAM_STEP
CHUNKS = 4
DIRECT_REPS = 8
MESH = pl.DeviceIdType.MESH
F32 = jnp.float32
BF16 = jnp.bfloat16


def from_behind(block, axis, distance):
    devices = range(lax.axis_size(axis))
    route = [((i - distance) % len(devices), i) for i in devices]
    return lax.ppermute(block, axis, route)


def gossip(values, offset, count_rep, wire):
    current = values
    for bit in range((count_rep - 1).bit_length()):
        span = (1 << bit) % count_rep
        digit = jnp.bitwise_and(jnp.right_shift(offset, bit), 1)
        moved = from_behind(current.astype(wire), "rep", span).astype(values.dtype)
        current = jnp.where(digit != 0, moved, current)
    return current


def partners(me, k, count):
    if count & (count - 1) == 0:
        other = me
        bit = 1
        while bit < count:
            if k & bit:
                other = other + bit * (1 - 2 * lax.rem(lax.div(me, bit), 2))
            bit *= 2
        return other, other
    return lax.rem(me + k, count), lax.rem(me + count - k, count)


def kernel(
    hop, count_rep, count, *refs
):
    (tok_hbm, og_hbm, gain_ref, inner_hbm, outer_hbm, mom_hbm, first_hbm, second_hbm), refs = refs[:8], refs[8:]
    outs, refs = refs[:4] if hop else refs[:3], refs[4:] if hop else refs[3:]
    (tok, tok_t, og, inner, outer, mom, first, second, w_all, out_buf, g_send, g_recv, g_own) = refs[:13]
    (load_sem, tok_sem, ag_send, ag_recv, rs_send, rs_recv, put_sem) = refs[13:20]
    if hop:
        outer_far, outer_out, delta_far, delta_out, far_send, far_recv, d_send, d_recv = refs[20:]

    me = lax.axis_index("fsdp")
    rows = inner.shape[0]
    part = rows // CHUNKS
    order = [k for k in range(1, count)]
    send_to = {k: partners(me, k, count)[0] for k in order}
    owner = {k: partners(me, k, count)[1] for k in order}
    owner[0] = me

    barrier = pltpu.get_barrier_semaphore()
    for k in order:
        pl.semaphore_signal(barrier, inc=1, device_id={"fsdp": owner[k]}, device_id_type=MESH)
    if hop:
        rep = lax.axis_index("rep")
        ahead = lax.rem(rep + hop, count_rep)
        behind = lax.rem(rep + count_rep - hop, count_rep)
        pl.semaphore_signal(barrier, inc=1, device_id={"rep": behind}, device_id_type=MESH)

    loads = [
        pltpu.make_async_copy(src, dst, load_sem.at[i])
        for i, (src, dst) in enumerate(
            [(inner_hbm, inner), (outer_hbm, outer), (og_hbm, og), (first_hbm, first), (second_hbm, second), (mom_hbm, mom)]
        )
    ]
    tok_loads = []
    for k in range(count):
        cols = pl.ds(pl.multiple_of(owner[k] * rows, rows), rows)
        tok_loads.append(pltpu.make_async_copy(tok_hbm.at[:, cols], tok.at[k], tok_sem.at[k]))
    loads[0].start()
    loads[1].start()
    for copy in tok_loads:
        copy.start()
    for copy in loads[2:]:
        copy.start()

    loads[0].wait()
    w_all[0] = inner[...].astype(BF16)
    pl.semaphore_wait(barrier, count if hop else count - 1)
    gathers = {}

    def gather(k, half, src, to):
        span = pl.ds(half * (rows // 2), rows // 2)
        gathers[k, half] = pltpu.make_async_remote_copy(
            src_ref=w_all.at[src, span, :],
            dst_ref=w_all.at[k, span, :],
            send_sem=ag_send.at[k, half],
            recv_sem=ag_recv.at[k, half],
            device_id={"fsdp": send_to[to]},
            device_id_type=MESH,
        )
        gathers[k, half].start()

    relayed = count == 4
    for half in range(2):
        for k in [1, 2] if relayed else reversed(order):
            gather(k, 1 - half if k == 1 else half, 0, k)
    loads[1].wait()
    if hop:
        outer_out[...] = outer[...].astype(BF16)
        far = pltpu.make_async_remote_copy(
            src_ref=outer_out,
            dst_ref=outer_far,
            send_sem=far_send.at[0],
            recv_sem=far_recv.at[0],
            device_id={"rep": ahead},
            device_id_type=MESH,
        )
        far.start()

    for k in range(count):
        tok_loads[k].wait()
        tok_t[k] = tok[k].T
    if relayed:
        gathers[2, 0].wait_recv()
        gather(3, 0, 2, 1)
        gathers[1, 1].wait_recv()
        gather(3, 1, 1, 2)
    for copy in loads[2:]:
        copy.wait()
    keys = jnp.dot(tok[0], w_all[0], preferred_element_type=F32)
    for k in order:
        for half in range(2):
            if not relayed or (k, half) not in ((2, 0), (1, 1)):
                gathers[k, half].wait_recv()
        keys = keys + jnp.dot(tok[k], w_all[k], preferred_element_type=F32)

    gain = gain_ref[...]
    pieces = []
    for h in range(keys.shape[1] // HEAD):
        head = keys[:, h * HEAD : (h + 1) * HEAD]
        scale = lax.rsqrt(jnp.mean(head * head, axis=-1, keepdims=True) + 1e-06)
        unit = head * scale
        g_out = og[:, h * HEAD : (h + 1) * HEAD].astype(F32) * gain
        inner_prod = jnp.mean(unit * g_out, axis=-1, keepdims=True)
        pieces.append((scale * (g_out - unit * inner_prod)).astype(BF16))
    key_grad = jnp.concatenate(pieces, axis=1)

    sums = {}

    def term_of(k, c):
        return jnp.dot(tok_t[k, pl.ds(c * part, part), :], key_grad, preferred_element_type=F32)

    def send_term(k, c, term, to):
        span = pl.ds(c * part, part)
        g_send[k - 1, span, :] = term.astype(BF16)
        sums[k, c] = pltpu.make_async_remote_copy(
            src_ref=g_send.at[k - 1, span, :],
            dst_ref=g_recv.at[k - 1, span, :],
            send_sem=rs_send.at[k - 1, c],
            recv_sem=rs_recv.at[k - 1, c],
            device_id={"fsdp": send_to[to]},
            device_id_type=MESH,
        )
        sums[k, c].start()

    def pass_on(c):
        k = 2 - c % 2
        term = term_of(k, c)
        sums[3, c].wait_recv()
        send_term(k, c, term + g_recv[2, pl.ds(c * part, part), :].astype(F32), k)

    if relayed:
        for c in range(CHUNKS + 1):
            if c < CHUNKS:
                send_term(3, c, term_of(3, c), 1 + c % 2)
            if c > 0:
                k = 1 + (c - 1) % 2
                send_term(k, c - 1, term_of(k, c - 1), k)
        pass_on(0)
        pass_on(1)
    else:
        for c in range(CHUNKS):
            for k in reversed(order):
                send_term(k, c, term_of(k, c), k)
    for c in range(CHUNKS):
        g_own[pl.ds(c * part, part), :] = term_of(0, c)

    puts = []

    def put(slot, c, values):
        span = pl.ds(c * part, part)
        out_buf[slot, span, :] = values
        copy = pltpu.make_async_copy(out_buf.at[slot, span, :], outs[slot].at[span, :], put_sem.at[slot, c])
        copy.start()
        puts.append(copy)

    hops = []
    for c in range(CHUNKS):
        span = pl.ds(c * part, part)
        if relayed and c + 2 < CHUNKS:
            pass_on(c + 2)
        grad = g_own[span, :]
        for k in [1, 2] if relayed else order:
            sums[k, c].wait_recv()
            grad = grad + g_recv[k - 1, span, :].astype(F32)
        first_new = 0.9 * first[span, :] + 0.1 * grad
        second_new = 0.95 * second[span, :] + 0.05 * grad * grad
        held = inner[span, :]
        update = first_new / FIX_ONE / (jnp.sqrt(second_new / FIX_TWO) + 1e-08) + 0.1 * held
        delta = outer[span, :] - (held - 0.05 * update)
        if hop:
            delta_out[span, :] = delta.astype(BF16)
            copy = pltpu.make_async_remote_copy(
                src_ref=delta_out.at[span, :],
                dst_ref=delta_far.at[span, :],
                send_sem=d_send.at[c],
                recv_sem=d_recv.at[c],
                device_id={"rep": ahead},
                device_id_type=MESH,
            )
            copy.start()
            hops.append(copy)
            g_own[span, :] = delta
        else:
            put(0, c, delta)
        put(len(outs) - 2, c, first_new)
        put(len(outs) - 1, c, second_new)

    if hop:
        far.wait_recv()
        for c in range(CHUNKS):
            span = pl.ds(c * part, part)
            hops[c].wait_recv()
            mean_delta = (g_own[span, :] + delta_far[span, :].astype(F32)) / 2.0
            momentum_new = 0.9 * mom[span, :] + mean_delta
            mid = (outer[span, :] + outer_far[span, :].astype(F32)) / 2.0
            put(1, c, momentum_new)
            put(0, c, mid - 0.7 * (0.9 * momentum_new + mean_delta))

    for k in order:
        for half in range(2):
            gathers[k, half].wait_send()
        for c in range(CHUNKS):
            sums[k, c].wait_send()
    if hop:
        far.wait_send()
        for copy in hops:
            copy.wait_send()
    for copy in puts:
        copy.wait()


def fused(hop, tokens, out_grad, gain, inner, outer, mom, first, second):
    count = lax.axis_size("fsdp")
    count_rep = lax.axis_size("rep")
    rows, width = inner.shape
    n_tok = tokens.shape[0]
    n_out = 4 if hop else 3
    full = lambda kind, *lead: pltpu.VMEM((*lead, rows, width), kind)
    dma = pltpu.SemaphoreType.DMA
    scratch = [
        pltpu.VMEM((count, n_tok, rows), BF16),
        pltpu.VMEM((count, rows, n_tok), BF16),
        pltpu.VMEM((n_tok, width), BF16),
        full(F32),
        full(F32),
        full(F32),
        full(F32),
        full(F32),
        full(BF16, count),
        full(F32, n_out),
        full(BF16, count - 1),
        full(BF16, count - 1),
        full(F32),
        dma((6,)),
        dma((count,)),
        dma((count, 2)),
        dma((count, 2)),
        dma((count - 1, CHUNKS)),
        dma((count - 1, CHUNKS)),
        dma((n_out, CHUNKS)),
    ]
    if hop:
        scratch += [full(BF16), full(BF16), full(BF16), full(BF16), dma((1,)), dma((1,)), dma((CHUNKS,)), dma((CHUNKS,))]
    hbm = pl.BlockSpec(memory_space=pl.ANY)
    return pl.pallas_call(
        functools.partial(kernel, hop, count_rep, count),
        out_shape=[jax.ShapeDtypeStruct((rows, width), F32)] * n_out,
        in_specs=[hbm, hbm, pl.BlockSpec(memory_space=pltpu.VMEM)] + [hbm] * 5,
        out_specs=[hbm] * n_out,
        scratch_shapes=scratch,
        cost_estimate=pl.CostEstimate(
            flops=4 * n_tok * rows * count * width, bytes_accessed=8 << 20, transcendentals=2 * rows * width
        ),
        compiler_params=pltpu.CompilerParams(
            collective_id=hop, has_side_effects=True, vmem_limit_bytes=48 << 20
        ),
        name=f"fused_hop{hop}",
    )(tokens, out_grad, gain, inner, outer, mom, first, second)


def drain(*refs):
    n = len(refs) // 2
    copies = [pltpu.make_async_copy(refs[i], refs[n + i], refs[-1].at[i]) for i in range(n)]
    for copy in copies:
        copy.start()
    for copy in copies:
        copy.wait()


def store(outs):
    hbm = pl.BlockSpec(memory_space=pl.ANY)
    return pl.pallas_call(
        drain,
        out_shape=[jax.ShapeDtypeStruct(out.shape, out.dtype) for out in outs],
        in_specs=[hbm] * len(outs),
        out_specs=[hbm] * len(outs),
        scratch_shapes=[pltpu.SemaphoreType.DMA((len(outs),))],
        name="store",
    )(*outs)


def local(
    tokens, out_grad, gain, inner_weight, outer_weight, momentum, adam_m, adam_v, gossip_offset
):
    count_rep = lax.axis_size("rep")
    code = gossip_offset[0] % (count_rep - 1)
    args = (tokens, out_grad, gain, inner_weight[0], outer_weight[0], momentum[0], adam_m[0], adam_v[0])
    if count_rep <= DIRECT_REPS:
        branches = [functools.partial(fused, hop) for hop in range(1, count_rep)]
        outs = store(lax.switch(code, branches, *args))
    else:
        offset = 1 + code
        outer = outer_weight[0]
        outer_far = gossip(outer, offset, count_rep, F32)
        delta, first_new, second_new = fused(0, *args)
        delta_far = gossip(delta, offset, count_rep, BF16)
        mean_delta = (delta + delta_far) / 2.0
        momentum_new = 0.9 * momentum[0] + mean_delta
        outer_new = (outer + outer_far) / 2.0 - 0.7 * (0.9 * momentum_new + mean_delta)
        outs = (outer_new, momentum_new, first_new, second_new)
    return tuple(out[None] for out in outs)


def solution(mesh):
    row = P("rep", "fsdp", None)
    both = P(("rep", "fsdp"), None)
    return jax.shard_map(
        local,
        mesh=mesh,
        in_specs=(both, both, P("rep", None), row, row, row, row, row, P()),
        out_specs=(row, row, row, row),
        check_vma=False,
    )
```
